512 devices in a mesh: ctx: 128 (over x, z, core), head: 4 (over y).
Axes of the slice: x: 4, y: 4, z: 16, core: 2. Of those that a mesh axis runs over, the one named last changes fastest.
Arguments:
- query: bfloat16 [32768, 20, 128], P('ctx', 'head'), may hold values from -12 to 12
- key: bfloat16 [32768, 20, 128], P('ctx', 'head'), may hold values from -12 to 12
- value: bfloat16 [32768, 20, 128], P('ctx', 'head'), may hold values from -6 to 6
- query_gain: float32 [20, 128], P('head'), may hold values from 0.1 to 1.9
- key_gain: float32 [20, 128], P('head'), may hold values from 0.1 to 1.9
- head_class: int32 [20], P('head'), may hold values from 0 to 1, as said below
- neighbours: int32 [128, 7], P('ctx'), may hold values from 0 to 127, as said below
- tiles: int32 [128, 7, 4, 4], P('ctx'), may hold values from 0 to 1, as said below
Outputs:
- attended: bfloat16 [32768, 20, 128], P('ctx', 'head')
The draws below stay inside these ranges and needn't reach their ends.
Inputs may be any that keep to these rules, and one draw needn't show every extreme that they name: `head_class`: each aligned group of 5 heads holds exactly 2 temporal heads. `neighbours`: entry 0 of frame f is f; every entry lies within 3 frames of f. For block 0, tiles with equal query and key tile are 1.
All inputs are finite; a program needn't handle non-finite values.
Results may differ from the reference program's by a relative error of at most 0.0081.
Values may be sent and summed in bfloat16 or wider, within the bound.
No kernel may reach another device: no remote copies, remote signals or barrier semaphores. Data moves between devices by JAX's collectives and lax.ppermute only.
A program may use at most 64 MiB of HBM per device.

```python
import jax
import jax.numpy as jnp
from jax import lax

HEADS = 20
HEAD_SIZE = 128
GROUP = 5
TEMP = 2
FRAME_POS = 256
NB = 7
TILE = 64
NT = 4
REACH = 3
FRAMES = 128
TOKENS = 32768
N_HEAD = 4


def head_scales():
    heads = jnp.arange(HEADS, dtype=jnp.float32)
    return 1.0 + 2.0 * heads / (HEADS - 1)


def draw_query(key, part):
    key = jax.random.fold_in(key, 11)
    body_vals = jnp.clip(jax.random.normal(key, (TOKENS, HEADS, HEAD_SIZE), jnp.float32), -3.5, 3.5)
    body_vals = body_vals * head_scales()[None, :, None]
    return body_vals.astype(jnp.bfloat16)


def draw_key(key, part):
    key = jax.random.fold_in(key, 12)
    body_vals = jnp.clip(jax.random.normal(key, (TOKENS, HEADS, HEAD_SIZE), jnp.float32), -3.5, 3.5)
    body_vals = body_vals * head_scales()[None, :, None]
    return body_vals.astype(jnp.bfloat16)


def draw_head_class(key, part):
    key = jax.random.fold_in(key, 13)
    keys = jax.random.split(key, N_HEAD)
    perms = jax.vmap(lambda k: jax.random.permutation(k, GROUP))(keys)
    return (perms < TEMP).astype(jnp.int32).reshape(HEADS)


def draw_neighbours(key, part):
    key = jax.random.fold_in(key, 14)
    slots = jnp.arange(2 * REACH, dtype=jnp.int32)
    offsets = jnp.where(slots < REACH, slots - REACH, slots - REACH + 1)
    keys = jax.random.split(key, FRAMES)
    perms = jax.vmap(lambda k: jax.random.permutation(k, 2 * REACH))(keys)
    chosen = jnp.take(offsets, perms[:, :NB - 1])
    frames = jnp.arange(FRAMES, dtype=jnp.int32)
    others = jnp.clip(frames[:, None] + chosen, 0, FRAMES - 1)
    return jnp.concatenate([frames[:, None], others], axis=1).astype(jnp.int32)


def draw_tiles(key, part):
    key = jax.random.fold_in(key, 15)
    level_key, bit_key = jax.random.split(key)
    level = jax.random.randint(level_key, (FRAMES, 1, 1, 1), 0, 4)
    bits = jax.random.randint(bit_key, (FRAMES, NB, NT, NT), 0, 20)
    on = (bits < 4 * (level + 1)).astype(jnp.int32)
    block = jnp.arange(NB, dtype=jnp.int32)[None, :, None, None]
    rows = jnp.arange(NT, dtype=jnp.int32)[None, None, :, None]
    cols = jnp.arange(NT, dtype=jnp.int32)[None, None, None, :]
    forced = (block == 0) & (rows == cols)
    return jnp.where(forced, 1, on).astype(jnp.int32)


def block_levels(key, shape, cuts, low, high):
    def one(dim, shards_of):
        steps = jax.random.uniform(jax.random.fold_in(jax.random.fold_in(key, 6), dim), (shards_of,), jnp.float32, low / len(cuts), high / len(cuts))
        return jnp.repeat(jnp.exp(steps), shape[dim] // shards_of).reshape((-1,) + (1,) * (len(shape) - dim - 1))

    factor_of = one(*cuts[0])
    for cut in cuts[1:]:
        factor_of = factor_of * one(*cut)
    return factor_of


def scatter_about(key, dims, spread, most, shards=(), kind=jnp.bfloat16):
    values = jax.random.normal(key, dims, jnp.float32) * spread
    if len(shards) > 0:
        values = block_levels(key, dims, shards, -0.22, 0.18) * values
    return jnp.clip(values, min=-most, max=most).astype(kind)


def setup_inputs(seed: int = 0) -> dict:
    key_of = jax.random.split(jax.random.key(seed), 9)
    return {
        "query": draw_query(jax.random.fold_in(key_of[8], 71), 0),
        "key": draw_key(jax.random.fold_in(key_of[8], 71), 0),
        "value": scatter_about(key_of[2], (TOKENS, HEADS, HEAD_SIZE), 1.0, 6.0, ((0, 128), (1, 4))),
        "query_gain": jnp.clip(1.0 + 0.18 * jax.random.normal(key_of[3], (HEADS, HEAD_SIZE), jnp.float32), 0.1, 1.9),
        "key_gain": jnp.clip(1.0 + 0.18 * jax.random.normal(key_of[4], (HEADS, HEAD_SIZE), jnp.float32), 0.1, 1.9),
        "head_class": draw_head_class(jax.random.fold_in(key_of[8], 71), 0),
        "neighbours": draw_neighbours(jax.random.fold_in(key_of[8], 71), 0),
        "tiles": draw_tiles(jax.random.fold_in(key_of[8], 71), 0),
    }


def normed(x, gain):
    xf = x.astype(jnp.float32)
    mean_sq = lax.optimization_barrier(jnp.mean(xf * xf, axis=(1, 2), keepdims=True))
    return (xf * lax.rsqrt(mean_sq + 1e-06) * gain[None]).astype(jnp.bfloat16)

def softened(scores):
    top = lax.optimization_barrier(jnp.max(scores, axis=-1, keepdims=True))
    expo = jnp.exp(scores - top)
    return (expo / lax.optimization_barrier(jnp.sum(expo, axis=-1, keepdims=True))).astype(jnp.bfloat16)

def expand_tiles(tile_rows):
    grown = jnp.repeat(jnp.repeat(tile_rows, TILE, axis=1), TILE, axis=2)
    grown = jnp.transpose(grown, (1, 0, 2))
    return grown.reshape(FRAME_POS, NB * FRAME_POS) > 0

def reference(query, key, value, query_gain, key_gain, head_class, neighbours, tiles):
    scale = HEAD_SIZE ** (-0.5)
    normed_query = normed(query, query_gain)
    normed_key = normed(key, key_gain)
    order = jnp.argsort(head_class, stable=True).astype(jnp.int32)
    n_spatial = HEADS - TEMP * N_HEAD
    spatial_heads = order[:n_spatial]
    temporal_heads = order[n_spatial:]
    shape4 = (FRAMES, FRAME_POS, HEADS, HEAD_SIZE)
    q_frames = normed_query.reshape(shape4)
    k_frames = normed_key.reshape(shape4)
    v_frames = value.reshape(shape4)
    q_spat = jnp.take(q_frames, spatial_heads, axis=2)
    k_spat = jnp.take(k_frames, spatial_heads, axis=2)
    v_spat = jnp.take(v_frames, spatial_heads, axis=2)

    def one_frame(items):
        q_rows, listed, tile_rows = items
        keys = jnp.take(k_spat, listed, axis=0).reshape(NB * FRAME_POS, n_spatial, HEAD_SIZE)
        vals = jnp.take(v_spat, listed, axis=0).reshape(NB * FRAME_POS, n_spatial, HEAD_SIZE)
        scores = jnp.einsum('qhd,khd->hqk', q_rows.astype(jnp.float32), keys.astype(jnp.float32)) * scale
        scores = jnp.where(expand_tiles(tile_rows)[None], scores, -jnp.inf)
        weights = softened(scores)
        return jnp.einsum('hqk,khd->qhd', weights.astype(jnp.float32), vals.astype(jnp.float32)).astype(jnp.bfloat16)
    spatial_out = lax.map(one_frame, (q_spat, neighbours, tiles))
    q_temp = jnp.moveaxis(jnp.take(q_frames, temporal_heads, axis=2), 1, 0)
    k_temp = jnp.moveaxis(jnp.take(k_frames, temporal_heads, axis=2), 1, 0)
    v_temp = jnp.moveaxis(jnp.take(v_frames, temporal_heads, axis=2), 1, 0)

    def one_position(items):
        q_rows, k_rows, v_rows = items
        scores = jnp.einsum('fhd,ghd->hfg', q_rows.astype(jnp.float32), k_rows.astype(jnp.float32)) * scale
        weights = softened(scores)
        return jnp.einsum('hfg,ghd->fhd', weights.astype(jnp.float32), v_rows.astype(jnp.float32)).astype(jnp.bfloat16)
    temporal_out = jnp.moveaxis(lax.map(one_position, (q_temp, k_temp, v_temp)), 0, 1)
    joined = jnp.concatenate([spatial_out, temporal_out], axis=2)
    inverse = jnp.argsort(order).astype(jnp.int32)
    attended = jnp.take(joined, inverse, axis=2)
    return attended.reshape(TOKENS, HEADS, HEAD_SIZE)
```

```python
import jax
import jax.numpy as jnp
from jax import lax
from jax.experimental import pallas as pl
from jax.experimental.pallas import tpu as pltpu
from jax.sharding import PartitionSpec as P

SIZE = 128
GROUP = 5
TEMP = 2
SPAT = GROUP - TEMP
POS = 256
NB = 7
TILE = 64
NT = 4
FRAMES = 128
HEADS = 20
LOG2E = 1.4426950408889634
SCALE = SIZE ** (-0.5) * LOG2E
UNSEEN = -1e30
BF16 = jnp.bfloat16
F32 = jnp.float32

SUB = POS // FRAMES


def whole(memory_space=pltpu.VMEM):
    return pl.BlockSpec(memory_space=memory_space)


def sorted_heads(class_ref):
    spat, temp = [0] * SPAT, [0] * TEMP
    n_spat, n_temp = 0, 0
    for head in range(GROUP):
        kind = class_ref[head]
        for r in range(SPAT):
            spat[r] = jnp.where((kind == 0) & (n_spat == r), head, spat[r])
        for r in range(TEMP):
            temp[r] = jnp.where((kind != 0) & (n_temp == r), head, temp[r])
        n_spat = n_spat + jnp.where(kind == 0, 1, 0)
        n_temp = n_temp + jnp.where(kind == 0, 0, 1)
    return spat, temp


def sums_kernel(q_ref, k_ref, sums_ref, q_buf, k_buf, sems):
    fetches = []
    for row, (x_ref, x_buf) in enumerate(((q_ref, q_buf), (k_ref, k_buf))):
        for head in range(GROUP):
            fetch = pltpu.make_async_copy(x_ref.at[head], x_buf.at[head], sems.at[row * GROUP + head])
            fetch.start()
            fetches.append(fetch)
    for row, x_buf in enumerate((q_buf, k_buf)):
        total = jnp.zeros((POS, SIZE), F32)
        for head in range(GROUP):
            fetches[row * GROUP + head].wait()
            part = x_buf[head].astype(F32)
            total = total + part * part
        sums_ref[row : row + 1] = jnp.sum(total.T, axis=0, keepdims=True)


def norm_kernel(class_ref, sums_ref, q_gain_ref, k_gain_ref, q_ref, k_ref, v_ref, qs_ref, kvs_ref, chunk_ref):
    spat, temp = sorted_heads(class_ref)
    factors = lax.rsqrt(sums_ref[...] / (HEADS * SIZE) + 1e-06)
    for row, (x_ref, gain_ref) in enumerate(((q_ref, q_gain_ref), (k_ref, k_gain_ref))):
        factor = jnp.broadcast_to(factors[row : row + 1], (SIZE, POS)).T

        def normed(head):
            return (x_ref[head].astype(F32) * factor * gain_ref[pl.ds(head, 1)]).astype(BF16)

        for r in range(TEMP):
            chunk_ref[:, row * TEMP + r] = normed(temp[r]).reshape(FRAMES, SUB, SIZE)
        for r in range(SPAT):
            if row == 0:
                qs_ref[r] = normed(spat[r])
            else:
                kvs_ref[0, r] = normed(spat[r])
    for r in range(TEMP):
        chunk_ref[:, 2 * TEMP + r] = v_ref[temp[r]].reshape(FRAMES, SUB, SIZE)
    for r in range(SPAT):
        kvs_ref[1, r] = v_ref[spat[r]]


def dot_t(a, b):
    return lax.dot_general(a, b, (((1,), (1,)), ((), ())), preferred_element_type=F32)


def attend(q, blocks, scores_ref, bias_of):
    top = None
    for w, (k, _) in enumerate(blocks):
        scores = bias_of(w, dot_t(q, k()) * SCALE)
        scores_ref[w] = scores
        block_top = jnp.maximum(scores[:, :SIZE], scores[:, SIZE:])
        top = block_top if top is None else jnp.maximum(top, block_top)
    top = jnp.max(top, axis=1, keepdims=True)
    total = jnp.zeros((POS, SIZE), F32)
    out = jnp.zeros((POS, SIZE), F32)
    for w, (_, v) in enumerate(blocks):
        expo = jnp.exp2(scores_ref[w] - top)
        total = total + expo[:, :SIZE] + expo[:, SIZE:]
        out = out + jnp.dot(expo.astype(BF16), v(), preferred_element_type=F32)
    return (out / jnp.sum(total, axis=1, keepdims=True)).astype(BF16)


def temporal_kernel(x_ref, y_ref):
    query_row = lax.broadcasted_iota(jnp.int32, (POS, POS), 0) % SUB
    key_row = lax.broadcasted_iota(jnp.int32, (POS, POS), 1) % SUB
    bias = jnp.where(query_row == key_row, 0.0, UNSEEN)
    for head in range(TEMP):
        q, k, v = (x_ref[:, t * TEMP + head].reshape(POS, SIZE) for t in range(3))
        scores = dot_t(q, k) * SCALE + bias
        expo = jnp.exp2(scores - jnp.max(scores, axis=1, keepdims=True))
        total = jnp.sum(expo, axis=1, keepdims=True)
        out = jnp.dot(expo.astype(BF16), v, preferred_element_type=F32) / total
        y_ref[:, head] = out.astype(BF16).reshape(FRAMES, SUB, SIZE)


def spatial_kernel(order_ref, bias_ref, q_ref, *refs):
    kv_refs, out_ref, scores_ref = refs[:NB], refs[NB], refs[NB + 1]

    def bias_of(w, scores):
        tiles = [
            scores[a * TILE : (a + 1) * TILE] + bias_ref[a : a + 1, w * POS : (w + 1) * POS] for a in range(NT)
        ]
        return jnp.concatenate(tiles, axis=0)

    blocks = [(lambda ref=ref: ref[0, 0], lambda ref=ref: ref[1, 0]) for ref in kv_refs]
    out_ref[0] = attend(q_ref[0], blocks, scores_ref, bias_of)


def join_kernel(order_ref, rows_ref, spatial_ref, out_ref):
    out_ref[0] = rows_ref[:, 0].reshape(POS, SIZE)


def route(block, target):
    pairs = [(i, target(i)) for i in range(FRAMES) if 0 <= target(i) < FRAMES]
    return lax.ppermute(block, "ctx", pairs)


def first_window(own):
    below = route(own, lambda i: i + 2)
    above = route(own, lambda i: i - 2)
    twin = route(own, lambda i: i ^ 1)
    return below, above, twin


def rest_window(own, below, above, twin):
    passed = jnp.where(lax.axis_index("ctx") % 2 == 1, below, above)
    far = route(passed, lambda i: i + 1 if i % 2 else i - 1)
    return [far, below, route(below, lambda i: i ^ 1), own, twin, above, route(above, lambda i: i ^ 1)]


EVEN = (-3, -2, -1, 0, 1, 2, 3)
ODD = (3, -2, -3, 0, -1, 2, 1)


def bias_rows(neighbours, tiles):
    frame = lax.axis_index("ctx")
    offsets = jnp.where(frame % 2 == 0, jnp.array(EVEN, jnp.int32), jnp.array(ODD, jnp.int32))
    listed = (neighbours[0][None, :] == (frame + offsets)[:, None]).astype(jnp.int32)
    times = jnp.sum(listed[:, :, None, None] * tiles[0][None], axis=1)
    bias = jnp.where(times > 0, jnp.log2(jnp.maximum(times, 1).astype(F32)), UNSEEN)
    bias = jnp.repeat(jnp.transpose(bias, (1, 0, 2)), TILE, axis=2)
    return bias.reshape(NT, NB * POS)


def head_order(head_class):
    heads = jnp.arange(GROUP, dtype=jnp.int32)
    rank_key = head_class * GROUP + heads
    rank = jnp.sum((rank_key[None, :] < rank_key[:, None]).astype(jnp.int32), axis=1)
    return jnp.sum(jnp.where(rank[:, None] == heads[None, :], heads[:, None], 0), axis=0)


def bf16(*dims):
    return jax.ShapeDtypeStruct(dims, BF16)


def params(mib=32):
    return pltpu.CompilerParams(vmem_limit_bytes=mib * 1024 * 1024)


def swap_all(block):
    return lax.all_to_all(block, "ctx", split_axis=0, concat_axis=0, tiled=True)


def shards(query, key, value, query_gain, key_gain, head_class, neighbours, tiles):
    q, k, v = (jnp.transpose(a, (1, 0, 2)) for a in (query, key, value))
    sums = pl.pallas_call(
        sums_kernel,
        out_shape=jax.ShapeDtypeStruct((2, POS), F32),
        in_specs=[whole(pl.ANY)] * 2,
        out_specs=whole(),
        scratch_shapes=[
            pltpu.VMEM((GROUP, POS, SIZE), BF16),
            pltpu.VMEM((GROUP, POS, SIZE), BF16),
            pltpu.SemaphoreType.DMA((2 * GROUP,)),
        ],
        compiler_params=params(60),
        name="sums",
    )(q, k)
    sums = lax.psum(sums, "head")
    q_own, kv_own, chunk = pl.pallas_call(
        norm_kernel,
        out_shape=(
            bf16(SPAT, POS, SIZE),
            bf16(2, SPAT, POS, SIZE),
            bf16(FRAMES, 3 * TEMP, SUB, SIZE),
        ),
        in_specs=[whole(pltpu.SMEM)] + [whole()] * 6,
        out_specs=(whole(),) * 3,
        compiler_params=params(16),
        name="norm",
    )(head_class, sums, query_gain, key_gain, q, k, v)
    rows = swap_all(chunk)
    first = first_window(kv_own)
    outputs = pl.pallas_call(
        temporal_kernel,
        out_shape=bf16(FRAMES, TEMP, SUB, SIZE),
        in_specs=[whole()],
        out_specs=whole(),
        compiler_params=params(16),
        name="temporal",
    )(rows)
    outputs, first = lax.optimization_barrier((outputs, first))
    temporal_out = swap_all(outputs)
    window = rest_window(kv_own, *first)

    order = head_order(head_class)
    bias = bias_rows(neighbours, tiles)
    head_block = pl.BlockSpec((1, POS, SIZE), lambda h, order_ref: (h, 0, 0))
    spatial = pl.pallas_call(
        spatial_kernel,
        out_shape=bf16(GROUP, POS, SIZE),
        grid_spec=pltpu.PrefetchScalarGridSpec(
            num_scalar_prefetch=1,
            grid=(SPAT,),
            in_specs=[pl.BlockSpec((NT, NB * POS), lambda h, order_ref: (0, 0))] + [head_block]
            + [pl.BlockSpec((2, 1, POS, SIZE), lambda h, order_ref: (0, h, 0, 0))] * NB,
            out_specs=pl.BlockSpec((1, POS, SIZE), lambda h, order_ref: (order_ref[h], 0, 0)),
            scratch_shapes=[pltpu.VMEM((NB, POS, POS), F32)],
        ),
        compiler_params=params(),
        name="spatial",
    )(order, bias, q_own, *window)
    out = pl.pallas_call(
        join_kernel,
        out_shape=bf16(GROUP, POS, SIZE),
        grid_spec=pltpu.PrefetchScalarGridSpec(
            num_scalar_prefetch=1,
            grid=(TEMP,),
            in_specs=[
                pl.BlockSpec((FRAMES, 1, SUB, SIZE), lambda h, order_ref: (0, h, 0, 0)),
                pl.BlockSpec(memory_space=pl.ANY),
            ],
            out_specs=pl.BlockSpec((1, POS, SIZE), lambda h, order_ref: (order_ref[SPAT + h], 0, 0)),
        ),
        input_output_aliases={2: 0},
        compiler_params=params(),
        name="join",
    )(order, temporal_out, spatial)
    return jnp.transpose(out, (1, 0, 2))


def solution(mesh):
    in_specs = (
        P("ctx", "head", None),
        P("ctx", "head", None),
        P("ctx", "head", None),
        P("head", None),
        P("head", None),
        P("head"),
        P("ctx", None),
        P("ctx", None, None, None),
    )
    out_specs = P("ctx", "head", None)
    return jax.shard_map(shards, mesh=mesh, in_specs=in_specs, out_specs=out_specs, check_vma=False)
```

```python
import jax
import jax.numpy as jnp
from jax import lax
from jax.experimental import pallas as pl
from jax.experimental.pallas import tpu as pltpu
from jax.sharding import PartitionSpec as P

SIZE = 128
GROUP = 5
TEMP = 2
SPAT = GROUP - TEMP
POS = 256
NB = 7
TILE = 64
NT = 4
FRAMES = 128
HEADS = 20
LOG2E = 1.4426950408889634
SCALE = SIZE ** (-0.5) * LOG2E
UNSEEN = -1e30
BF16 = jnp.bfloat16
F32 = jnp.float32

SUB = POS // FRAMES


def whole(memory_space=pltpu.VMEM):
    return pl.BlockSpec(memory_space=memory_space)


def sorted_heads(class_ref):
    spat, temp = [0] * SPAT, [0] * TEMP
    n_spat, n_temp = 0, 0
    for head in range(GROUP):
        kind = class_ref[head]
        for r in range(SPAT):
            spat[r] = jnp.where((kind == 0) & (n_spat == r), head, spat[r])
        for r in range(TEMP):
            temp[r] = jnp.where((kind != 0) & (n_temp == r), head, temp[r])
        n_spat = n_spat + jnp.where(kind == 0, 1, 0)
        n_temp = n_temp + jnp.where(kind == 0, 0, 1)
    return spat, temp


def sums_kernel(q_ref, k_ref, sums_ref, q_buf, k_buf, sems):
    fetches = []
    for row, (x_ref, x_buf) in enumerate(((q_ref, q_buf), (k_ref, k_buf))):
        for head in range(GROUP):
            fetch = pltpu.make_async_copy(x_ref.at[head], x_buf.at[head], sems.at[row * GROUP + head])
            fetch.start()
            fetches.append(fetch)
    for row, x_buf in enumerate((q_buf, k_buf)):
        total = jnp.zeros((POS, SIZE), F32)
        for head in range(GROUP):
            fetches[row * GROUP + head].wait()
            part = x_buf[head].astype(F32)
            total = total + part * part
        sums_ref[row : row + 1] = jnp.sum(total.T, axis=0, keepdims=True)


def fetched(refs, heads, buf_ref, sems):
    fetches = []
    for t, x_ref in enumerate(refs):
        for r, head in enumerate(heads):
            place = t * len(heads) + r
            fetches.append(pltpu.make_async_copy(x_ref.at[head], buf_ref.at[place], sems.at[place]))
            fetches[-1].start()
    return fetches


def factors_of(sums_ref):
    factors = lax.rsqrt(sums_ref[...] / (HEADS * SIZE) + 1e-06)
    return [jnp.broadcast_to(factors[row : row + 1], (SIZE, POS)).T for row in range(2)]


def norm_kernel(
    class_ref, sums_ref, q_gain_ref, k_gain_ref, q_ref, k_ref, v_ref, qs_ref, kvs_ref, chunk_ref, buf_ref, sems
):
    spat, temp = sorted_heads(class_ref)
    heads = spat + temp
    fetches = fetched((k_ref, v_ref, q_ref), heads, buf_ref, sems)
    factors = factors_of(sums_ref)
    for place, fetch in enumerate(fetches):
        t, r = divmod(place, GROUP)
        fetch.wait()
        rows = buf_ref[place]
        if t != 1:
            gain = (k_gain_ref, None, q_gain_ref)[t][pl.ds(heads[r], 1)]
            rows = (rows.astype(F32) * factors[1 - t // 2] * gain).astype(BF16)
        if r >= SPAT:
            chunk_ref[:, (1, 2, 0)[t] * TEMP + r - SPAT] = rows.reshape(FRAMES, SUB, SIZE)
        elif t < 2:
            kvs_ref[t, r] = rows
        else:
            qs_ref[r] = rows


def dot_t(a, b):
    return lax.dot_general(a, b, (((1,), (1,)), ((), ())), preferred_element_type=F32)


def attend(q, blocks, scores_ref, bias_of):
    top = None
    for w, (k, _) in enumerate(blocks):
        scores = bias_of(w, dot_t(q, k()) * SCALE)
        scores_ref[w] = scores
        block_top = jnp.maximum(scores[:, :SIZE], scores[:, SIZE:])
        top = block_top if top is None else jnp.maximum(top, block_top)
    top = jnp.max(top, axis=1, keepdims=True)
    total = jnp.zeros((POS, SIZE), F32)
    out = jnp.zeros((POS, SIZE), F32)
    for w, (_, v) in enumerate(blocks):
        expo = jnp.exp2(scores_ref[w] - top)
        total = total + expo[:, :SIZE] + expo[:, SIZE:]
        out = out + jnp.dot(expo.astype(BF16), v(), preferred_element_type=F32)
    return (out / jnp.sum(total, axis=1, keepdims=True)).astype(BF16)


def temporal_kernel(x_ref, y_ref):
    query_row = lax.broadcasted_iota(jnp.int32, (POS, POS), 0) % SUB
    key_row = lax.broadcasted_iota(jnp.int32, (POS, POS), 1) % SUB
    bias = jnp.where(query_row == key_row, 0.0, UNSEEN)
    for head in range(TEMP):
        q, k, v = (x_ref[:, t * TEMP + head].reshape(POS, SIZE) for t in range(3))
        scores = dot_t(q, k) * SCALE + bias
        expo = jnp.exp2(scores - jnp.max(scores, axis=1, keepdims=True))
        total = jnp.sum(expo, axis=1, keepdims=True)
        out = jnp.dot(expo.astype(BF16), v, preferred_element_type=F32) / total
        y_ref[:, head] = out.astype(BF16).reshape(FRAMES, SUB, SIZE)


def spatial_kernel(order_ref, bias_ref, q_ref, *refs):
    kv_refs, (out_ref, scores_ref, rows_ref, sems) = refs[:NB], refs[NB:]

    def bias_of(w, scores):
        tiles = [
            scores[a * TILE : (a + 1) * TILE] + bias_ref[a : a + 1, w * POS : (w + 1) * POS] for a in range(NT)
        ]
        return jnp.concatenate(tiles, axis=0)

    copies = []
    for head in range(SPAT):
        blocks = [(lambda ref=ref: ref[0, head], lambda ref=ref: ref[1, head]) for ref in kv_refs]
        rows_ref[head] = attend(q_ref[head], blocks, scores_ref, bias_of)
        copies.append(pltpu.make_async_copy(rows_ref.at[head], out_ref.at[order_ref[head]], sems.at[head]))
        copies[-1].start()
    for copy in copies:
        copy.wait()


def join_kernel(order_ref, moved_ref, spatial_ref, out_ref, rows_ref, sems):
    copies = []
    for head in range(TEMP):
        rows_ref[head] = moved_ref[:, head].reshape(POS, SIZE)
        place = order_ref[SPAT + head]
        copies.append(pltpu.make_async_copy(rows_ref.at[head], out_ref.at[place], sems.at[head]))
        copies[-1].start()
    for copy in copies:
        copy.wait()


def route(block, target):
    pairs = [(i, target(i)) for i in range(FRAMES) if 0 <= target(i) < FRAMES]
    return lax.ppermute(block, "ctx", pairs)


def first_window(own):
    below = route(own, lambda i: i + 2)
    above = route(own, lambda i: i - 2)
    twin = route(own, lambda i: i ^ 1)
    return below, above, twin


def rest_window(own, below, above, twin):
    passed = jnp.where(lax.axis_index("ctx") % 2 == 1, below, above)
    passed, below, above = lax.optimization_barrier((passed, below, above))
    far = route(passed, lambda i: i + 1 if i % 2 else i - 1)
    return [far, below, route(below, lambda i: i ^ 1), own, twin, above, route(above, lambda i: i ^ 1)]


EVEN = (-3, -2, -1, 0, 1, 2, 3)
ODD = (3, -2, -3, 0, -1, 2, 1)


def bias_rows(neighbours, tiles):
    frame = lax.axis_index("ctx")
    offsets = jnp.where(frame % 2 == 0, jnp.array(EVEN, jnp.int32), jnp.array(ODD, jnp.int32))
    listed = (neighbours[0][None, :] == (frame + offsets)[:, None]).astype(jnp.int32)
    times = jnp.sum(listed[:, :, None, None] * tiles[0][None], axis=1)
    bias = jnp.where(times > 0, jnp.log2(jnp.maximum(times, 1).astype(F32)), UNSEEN)
    bias = jnp.repeat(jnp.transpose(bias, (1, 0, 2)), TILE, axis=2)
    return bias.reshape(NT, NB * POS)


def head_order(head_class):
    heads = jnp.arange(GROUP, dtype=jnp.int32)
    rank_key = head_class * GROUP + heads
    rank = jnp.sum((rank_key[None, :] < rank_key[:, None]).astype(jnp.int32), axis=1)
    return jnp.sum(jnp.where(rank[:, None] == heads[None, :], heads[:, None], 0), axis=0)


def bf16(*dims):
    return jax.ShapeDtypeStruct(dims, BF16)


def params(mib=32):
    return pltpu.CompilerParams(vmem_limit_bytes=mib * 1024 * 1024)


def swap_all(block):
    return lax.all_to_all(block, "ctx", split_axis=0, concat_axis=0, tiled=True)


def shards(query, key, value, query_gain, key_gain, head_class, neighbours, tiles):
    q, k, v = (jnp.transpose(a, (1, 0, 2)) for a in (query, key, value))
    sums = pl.pallas_call(
        sums_kernel,
        out_shape=jax.ShapeDtypeStruct((2, POS), F32),
        in_specs=[whole(pl.ANY)] * 2,
        out_specs=whole(),
        scratch_shapes=[
            pltpu.VMEM((GROUP, POS, SIZE), BF16),
            pltpu.VMEM((GROUP, POS, SIZE), BF16),
            pltpu.SemaphoreType.DMA((2 * GROUP,)),
        ],
        compiler_params=params(60),
        name="sums",
    )(q, k)
    sums = lax.psum(sums, "head")
    q_own, kv_own, chunk = pl.pallas_call(
        norm_kernel,
        out_shape=(
            bf16(SPAT, POS, SIZE),
            bf16(2, SPAT, POS, SIZE),
            bf16(FRAMES, 3 * TEMP, SUB, SIZE),
        ),
        in_specs=[whole(pltpu.SMEM)] + [whole()] * 3 + [whole(pl.ANY)] * 3,
        out_specs=(whole(),) * 3,
        scratch_shapes=[pltpu.VMEM((3 * GROUP, POS, SIZE), BF16), pltpu.SemaphoreType.DMA((3 * GROUP,))],
        compiler_params=params(60),
        name="norm",
    )(head_class, sums, query_gain, key_gain, q, k, v)
    rows = swap_all(chunk)
    first = first_window(kv_own)
    outputs = pl.pallas_call(
        temporal_kernel,
        out_shape=bf16(FRAMES, TEMP, SUB, SIZE),
        in_specs=[whole()],
        out_specs=whole(),
        compiler_params=params(16),
        name="temporal",
    )(rows)
    outputs, first = lax.optimization_barrier((outputs, first))
    temporal_out = swap_all(outputs)
    window = rest_window(kv_own, *first)

    order = head_order(head_class)
    bias = bias_rows(neighbours, tiles)
    smem = whole(pltpu.SMEM)
    spatial = pl.pallas_call(
        spatial_kernel,
        out_shape=bf16(GROUP, POS, SIZE),
        in_specs=[smem] + [whole()] * (2 + NB),
        out_specs=whole(pl.ANY),
        scratch_shapes=[
            pltpu.VMEM((NB, POS, POS), F32),
            pltpu.VMEM((SPAT, POS, SIZE), BF16),
            pltpu.SemaphoreType.DMA((SPAT,)),
        ],
        compiler_params=params(16),
        name="spatial",
    )(order, bias, q_own, *window)
    out = pl.pallas_call(
        join_kernel,
        out_shape=bf16(GROUP, POS, SIZE),
        in_specs=[smem, whole(), whole(pl.ANY)],
        out_specs=whole(pl.ANY),
        scratch_shapes=[pltpu.VMEM((TEMP, POS, SIZE), BF16), pltpu.SemaphoreType.DMA((TEMP,))],
        input_output_aliases={2: 0},
        compiler_params=params(16),
        name="join",
    )(order, temporal_out, spatial)
    return jnp.transpose(out, (1, 0, 2))


def solution(mesh):
    in_specs = (
        P("ctx", "head", None),
        P("ctx", "head", None),
        P("ctx", "head", None),
        P("head", None),
        P("head", None),
        P("head"),
        P("ctx", None),
        P("ctx", None, None, None),
    )
    out_specs = P("ctx", "head", None)
    return jax.shard_map(shards, mesh=mesh, in_specs=in_specs, out_specs=out_specs, check_vma=False)
```

```python
import jax
import jax.numpy as jnp
from jax import lax
from jax.experimental import pallas as pl
from jax.experimental.pallas import tpu as pltpu
from jax.sharding import PartitionSpec as P

SIZE = 128
GROUP = 5
TEMP = 2
SPAT = GROUP - TEMP
POS = 256
NB = 7
TILE = 64
NT = 4
FRAMES = 128
HEADS = 20
LOG2E = 1.4426950408889634
SCALE = SIZE ** (-0.5) * LOG2E
UNSEEN = -1e30
BF16 = jnp.bfloat16
F32 = jnp.float32

SUB = POS // FRAMES


def whole(memory_space=pltpu.VMEM):
    return pl.BlockSpec(memory_space=memory_space)


def sorted_heads(class_ref):
    spat, temp = [0] * SPAT, [0] * TEMP
    n_spat, n_temp = 0, 0
    for head in range(GROUP):
        kind = class_ref[head]
        for r in range(SPAT):
            spat[r] = jnp.where((kind == 0) & (n_spat == r), head, spat[r])
        for r in range(TEMP):
            temp[r] = jnp.where((kind != 0) & (n_temp == r), head, temp[r])
        n_spat = n_spat + jnp.where(kind == 0, 1, 0)
        n_temp = n_temp + jnp.where(kind == 0, 0, 1)
    return spat, temp


def sums_kernel(q_ref, k_ref, sums_ref, q_buf, k_buf, sems):
    half = POS // 2
    fetches = []
    for row, (x_ref, x_buf) in enumerate(((q_ref, q_buf), (k_ref, k_buf))):
        for head in range(GROUP):
            for part in range(2):
                rows = pl.ds(part * half, half)
                sem = sems.at[(row * GROUP + head) * 2 + part]
                fetches.append(pltpu.make_async_copy(x_ref.at[head, rows], x_buf.at[head, rows], sem))
                fetches[-1].start()
    for row, x_buf in enumerate((q_buf, k_buf)):
        total = jnp.zeros((POS, SIZE), F32)
        for head in range(GROUP):
            for part in range(2):
                fetches[(row * GROUP + head) * 2 + part].wait()
            part = x_buf[head].astype(F32)
            total = total + part * part
        sums_ref[row : row + 1] = jnp.sum(total.T, axis=0, keepdims=True)


def fetched(refs, heads, buf_ref, sems):
    fetches = []
    for t, x_ref in enumerate(refs):
        for r, head in enumerate(heads):
            place = t * len(heads) + r
            fetches.append(pltpu.make_async_copy(x_ref.at[head], buf_ref.at[place], sems.at[place]))
            fetches[-1].start()
    return fetches


def factors_of(sums_ref):
    factors = lax.rsqrt(sums_ref[...] / (HEADS * SIZE) + 1e-06)
    return [jnp.broadcast_to(factors[row : row + 1], (SIZE, POS)).T for row in range(2)]


def norm_temporal_kernel(class_ref, sums_ref, q_gain_ref, k_gain_ref, q_ref, k_ref, v_ref, chunk_ref, buf_ref, sems):
    _, temp = sorted_heads(class_ref)
    fetches = fetched((q_ref, k_ref, v_ref), temp, buf_ref, sems)
    factors = factors_of(sums_ref)
    for place, fetch in enumerate(fetches):
        t, r = divmod(place, TEMP)
        fetch.wait()
        rows = buf_ref[place]
        if t < 2:
            gain = (q_gain_ref, k_gain_ref)[t][pl.ds(temp[r], 1)]
            rows = (rows.astype(F32) * factors[t] * gain).astype(BF16)
        chunk_ref[:, place] = rows.reshape(FRAMES, SUB, SIZE)


def norm_spatial_kernel(
    class_ref, sums_ref, q_gain_ref, k_gain_ref, q_ref, k_ref, v_ref, qs_ref, kvs_ref, buf_ref, sems
):
    spat, _ = sorted_heads(class_ref)
    fetches = fetched((q_ref, k_ref, v_ref), spat, buf_ref, sems)
    factors = factors_of(sums_ref)
    for place, fetch in enumerate(fetches):
        t, r = divmod(place, SPAT)
        fetch.wait()
        rows = buf_ref[place]
        if t < 2:
            gain = (q_gain_ref, k_gain_ref)[t][pl.ds(spat[r], 1)]
            rows = (rows.astype(F32) * factors[t] * gain).astype(BF16)
        if t == 0:
            qs_ref[r] = rows
        else:
            kvs_ref[t - 1, r] = rows


def dot_t(a, b):
    return lax.dot_general(a, b, (((1,), (1,)), ((), ())), preferred_element_type=F32)


def attend(q, blocks, scores_ref, bias_of):
    top = None
    for w, (k, _) in enumerate(blocks):
        scores = bias_of(w, dot_t(q, k()) * SCALE)
        scores_ref[w] = scores
        block_top = jnp.maximum(scores[:, :SIZE], scores[:, SIZE:])
        top = block_top if top is None else jnp.maximum(top, block_top)
    top = jnp.max(top, axis=1, keepdims=True)
    total = jnp.zeros((POS, SIZE), F32)
    out = jnp.zeros((POS, SIZE), F32)
    for w, (_, v) in enumerate(blocks):
        expo = jnp.exp2(scores_ref[w] - top)
        total = total + expo[:, :SIZE] + expo[:, SIZE:]
        out = out + jnp.dot(expo.astype(BF16), v(), preferred_element_type=F32)
    return (out / jnp.sum(total, axis=1, keepdims=True)).astype(BF16)


def temporal_kernel(x_ref, y_ref):
    query_row = lax.broadcasted_iota(jnp.int32, (POS, POS), 0) % SUB
    key_row = lax.broadcasted_iota(jnp.int32, (POS, POS), 1) % SUB
    bias = jnp.where(query_row == key_row, 0.0, UNSEEN)
    for head in range(TEMP):
        q, k, v = (x_ref[:, t * TEMP + head].reshape(POS, SIZE) for t in range(3))
        scores = dot_t(q, k) * SCALE + bias
        expo = jnp.exp2(scores - jnp.max(scores, axis=1, keepdims=True))
        total = jnp.sum(expo, axis=1, keepdims=True)
        out = jnp.dot(expo.astype(BF16), v, preferred_element_type=F32) / total
        y_ref[:, head] = out.astype(BF16).reshape(FRAMES, SUB, SIZE)


def spatial_kernel(order_ref, bias_ref, q_ref, *refs):
    kv_refs, (out_ref, scores_ref, rows_ref, sems) = refs[:NB], refs[NB:]

    def bias_of(w, scores):
        tiles = [
            scores[a * TILE : (a + 1) * TILE] + bias_ref[a : a + 1, w * POS : (w + 1) * POS] for a in range(NT)
        ]
        return jnp.concatenate(tiles, axis=0)

    copies = []
    for head in range(SPAT):
        blocks = [(lambda ref=ref: ref[0, head], lambda ref=ref: ref[1, head]) for ref in kv_refs]
        rows_ref[head] = attend(q_ref[head], blocks, scores_ref, bias_of)
        copies.append(pltpu.make_async_copy(rows_ref.at[head], out_ref.at[order_ref[head]], sems.at[head]))
        copies[-1].start()
    for copy in copies:
        copy.wait()


def join_kernel(order_ref, moved_ref, spatial_ref, out_ref, rows_ref, sems):
    copies = []
    for head in range(TEMP):
        rows_ref[head] = moved_ref[:, head].reshape(POS, SIZE)
        place = order_ref[SPAT + head]
        copies.append(pltpu.make_async_copy(rows_ref.at[head], out_ref.at[place], sems.at[head]))
        copies[-1].start()
    for copy in copies:
        copy.wait()


def route(block, target):
    pairs = [(i, target(i)) for i in range(FRAMES) if 0 <= target(i) < FRAMES]
    return lax.ppermute(block, "ctx", pairs)


def first_window(own):
    below = route(own, lambda i: i + 2)
    above = route(own, lambda i: i - 2)
    twin = route(own, lambda i: i ^ 1)
    return below, above, twin


def rest_window(own, below, above, twin):
    passed = jnp.where(lax.axis_index("ctx") % 2 == 1, below, above)
    passed, below, above = lax.optimization_barrier((passed, below, above))
    far = route(passed, lambda i: i + 1 if i % 2 else i - 1)
    return [far, below, route(below, lambda i: i ^ 1), own, twin, above, route(above, lambda i: i ^ 1)]


EVEN = (-3, -2, -1, 0, 1, 2, 3)
ODD = (3, -2, -3, 0, -1, 2, 1)


def bias_rows(neighbours, tiles):
    frame = lax.axis_index("ctx")
    offsets = jnp.where(frame % 2 == 0, jnp.array(EVEN, jnp.int32), jnp.array(ODD, jnp.int32))
    listed = (neighbours[0][None, :] == (frame + offsets)[:, None]).astype(jnp.int32)
    times = jnp.sum(listed[:, :, None, None] * tiles[0][None], axis=1)
    bias = jnp.where(times > 0, jnp.log2(jnp.maximum(times, 1).astype(F32)), UNSEEN)
    bias = jnp.repeat(jnp.transpose(bias, (1, 0, 2)), TILE, axis=2)
    return bias.reshape(NT, NB * POS)


def head_order(head_class):
    heads = jnp.arange(GROUP, dtype=jnp.int32)
    rank_key = head_class * GROUP + heads
    rank = jnp.sum((rank_key[None, :] < rank_key[:, None]).astype(jnp.int32), axis=1)
    return jnp.sum(jnp.where(rank[:, None] == heads[None, :], heads[:, None], 0), axis=0)


def bf16(*dims):
    return jax.ShapeDtypeStruct(dims, BF16)


def params(mib=32):
    return pltpu.CompilerParams(vmem_limit_bytes=mib * 1024 * 1024)


def swap_all(block):
    return lax.all_to_all(block, "ctx", split_axis=0, concat_axis=0, tiled=True)


def shards(query, key, value, query_gain, key_gain, head_class, neighbours, tiles):
    q, k, v = (jnp.transpose(a, (1, 0, 2)) for a in (query, key, value))
    sums = pl.pallas_call(
        sums_kernel,
        out_shape=jax.ShapeDtypeStruct((2, POS), F32),
        in_specs=[whole(pl.ANY)] * 2,
        out_specs=whole(),
        scratch_shapes=[
            pltpu.VMEM((GROUP, POS, SIZE), BF16),
            pltpu.VMEM((GROUP, POS, SIZE), BF16),
            pltpu.SemaphoreType.DMA((4 * GROUP,)),
        ],
        compiler_params=params(60),
        name="sums",
    )(q, k)
    sums = lax.psum(sums, "head")
    norm_specs = [whole(pltpu.SMEM)] + [whole()] * 3 + [whole(pl.ANY)] * 3
    chunk = pl.pallas_call(
        norm_temporal_kernel,
        out_shape=bf16(FRAMES, 3 * TEMP, SUB, SIZE),
        in_specs=norm_specs,
        out_specs=whole(),
        scratch_shapes=[pltpu.VMEM((3 * TEMP, POS, SIZE), BF16), pltpu.SemaphoreType.DMA((3 * TEMP,))],
        compiler_params=params(60),
        name="norm_temporal",
    )(head_class, sums, query_gain, key_gain, q, k, v)
    chunk, sums = lax.optimization_barrier((chunk, sums))
    rows = swap_all(chunk)
    q_own, kv_own = pl.pallas_call(
        norm_spatial_kernel,
        out_shape=(bf16(SPAT, POS, SIZE), bf16(2, SPAT, POS, SIZE)),
        in_specs=norm_specs,
        out_specs=(whole(),) * 2,
        scratch_shapes=[pltpu.VMEM((3 * SPAT, POS, SIZE), BF16), pltpu.SemaphoreType.DMA((3 * SPAT,))],
        compiler_params=params(16),
        name="norm_spatial",
    )(head_class, sums, query_gain, key_gain, q, k, v)
    first = first_window(kv_own)
    outputs = pl.pallas_call(
        temporal_kernel,
        out_shape=bf16(FRAMES, TEMP, SUB, SIZE),
        in_specs=[whole()],
        out_specs=whole(),
        compiler_params=params(16),
        name="temporal",
    )(rows)
    outputs, first = lax.optimization_barrier((outputs, first))
    temporal_out = swap_all(outputs)
    window = rest_window(kv_own, *first)

    order = head_order(head_class)
    bias = bias_rows(neighbours, tiles)
    smem = whole(pltpu.SMEM)
    spatial = pl.pallas_call(
        spatial_kernel,
        out_shape=bf16(GROUP, POS, SIZE),
        in_specs=[smem] + [whole()] * (2 + NB),
        out_specs=whole(pl.ANY),
        scratch_shapes=[
            pltpu.VMEM((NB, POS, POS), F32),
            pltpu.VMEM((SPAT, POS, SIZE), BF16),
            pltpu.SemaphoreType.DMA((SPAT,)),
        ],
        compiler_params=params(16),
        name="spatial",
    )(order, bias, q_own, *window)
    out = pl.pallas_call(
        join_kernel,
        out_shape=bf16(GROUP, POS, SIZE),
        in_specs=[smem, whole(), whole(pl.ANY)],
        out_specs=whole(pl.ANY),
        scratch_shapes=[pltpu.VMEM((TEMP, POS, SIZE), BF16), pltpu.SemaphoreType.DMA((TEMP,))],
        input_output_aliases={2: 0},
        compiler_params=params(16),
        name="join",
    )(order, temporal_out, spatial)
    return jnp.transpose(out, (1, 0, 2))


def solution(mesh):
    in_specs = (
        P("ctx", "head", None),
        P("ctx", "head", None),
        P("ctx", "head", None),
        P("head", None),
        P("head", None),
        P("head"),
        P("ctx", None),
        P("ctx", None, None, None),
    )
    out_specs = P("ctx", "head", None)
    return jax.shard_map(shards, mesh=mesh, in_specs=in_specs, out_specs=out_specs, check_vma=False)
```

```python
import jax
import jax.numpy as jnp
from jax import lax
from jax.experimental import pallas as pl
from jax.experimental.pallas import tpu as pltpu
from jax.sharding import PartitionSpec as P

SIZE = 128
GROUP = 5
TEMP = 2
SPAT = GROUP - TEMP
POS = 256
NB = 7
TILE = 64
NT = 4
FRAMES = 128
HEADS = 20
LOG2E = 1.4426950408889634
SCALE = SIZE ** (-0.5) * LOG2E
UNSEEN = -1e30
BF16 = jnp.bfloat16
F32 = jnp.float32

SUB = POS // FRAMES


def whole(memory_space=pltpu.VMEM):
    return pl.BlockSpec(memory_space=memory_space)


def sorted_heads(class_ref):
    spat, temp = [0] * SPAT, [0] * TEMP
    n_spat, n_temp = 0, 0
    for head in range(GROUP):
        kind = class_ref[head]
        for r in range(SPAT):
            spat[r] = jnp.where((kind == 0) & (n_spat == r), head, spat[r])
        for r in range(TEMP):
            temp[r] = jnp.where((kind != 0) & (n_temp == r), head, temp[r])
        n_spat = n_spat + jnp.where(kind == 0, 1, 0)
        n_temp = n_temp + jnp.where(kind == 0, 0, 1)
    return spat, temp


def sums_kernel(q_ref, k_ref, sums_ref, q_buf, k_buf, sems):
    half = POS // 2
    fetches = []
    for row, (x_ref, x_buf) in enumerate(((q_ref, q_buf), (k_ref, k_buf))):
        for head in range(GROUP):
            for part in range(2):
                rows = pl.ds(part * half, half)
                sem = sems.at[(row * GROUP + head) * 2 + part]
                fetches.append(pltpu.make_async_copy(x_ref.at[head, rows], x_buf.at[head, rows], sem))
                fetches[-1].start()
    for row, x_buf in enumerate((q_buf, k_buf)):
        total = jnp.zeros((POS, SIZE), F32)
        for head in range(GROUP):
            for part in range(2):
                fetches[(row * GROUP + head) * 2 + part].wait()
            part = x_buf[head].astype(F32)
            total = total + part * part
        sums_ref[row : row + 1] = jnp.sum(total.T, axis=0, keepdims=True)


def fetched(refs, heads, buf_ref, sems):
    fetches = []
    for t, x_ref in enumerate(refs):
        for r, head in enumerate(heads):
            place = t * len(heads) + r
            fetches.append(pltpu.make_async_copy(x_ref.at[head], buf_ref.at[place], sems.at[place]))
            fetches[-1].start()
    return fetches


def factors_of(sums_ref):
    factors = lax.rsqrt(sums_ref[...] / (HEADS * SIZE) + 1e-06)
    return [jnp.broadcast_to(factors[row : row + 1], (SIZE, POS)).T for row in range(2)]


def norm_temporal_kernel(
    class_ref, sums_hbm, q_gain_hbm, k_gain_hbm, q_ref, k_ref, v_ref, out_ref,
    sums_ref, q_gain_ref, k_gain_ref, buf_ref, chunk_ref, sems, small_sems, out_sems
):
    small = []
    for i, (src, dst) in enumerate(
        ((sums_hbm, sums_ref), (q_gain_hbm, q_gain_ref), (k_gain_hbm, k_gain_ref))
    ):
        small.append(pltpu.make_async_copy(src, dst, small_sems.at[i]))
        small[-1].start()
    _, temp = sorted_heads(class_ref)
    fetches = fetched((q_ref, k_ref, v_ref), temp, buf_ref, sems)
    for copy in small:
        copy.wait()
    factors = factors_of(sums_ref)
    sends = []
    for t in (2, 0, 1):
        for r in range(TEMP):
            place = t * TEMP + r
            fetches[place].wait()
            rows = buf_ref[place]
            if t < 2:
                gain = (q_gain_ref, k_gain_ref)[t][pl.ds(temp[r], 1)]
                rows = (rows.astype(F32) * factors[t] * gain).astype(BF16)
            chunk_ref[t, :, r] = rows.reshape(FRAMES, SUB, SIZE)
        sends.append(
            pltpu.make_async_copy(chunk_ref.at[t], out_ref.at[:, pl.ds(t * TEMP, TEMP)], out_sems.at[t])
        )
        sends[-1].start()
    for send in sends:
        send.wait()


def norm_spatial_kernel(
    class_ref, sums_ref, q_gain_ref, k_gain_ref, q_ref, k_ref, v_ref, qs_ref, kvs_ref, buf_ref, sems
):
    spat, _ = sorted_heads(class_ref)
    fetches = fetched((q_ref, k_ref, v_ref), spat, buf_ref, sems)
    factors = factors_of(sums_ref)
    for place, fetch in enumerate(fetches):
        t, r = divmod(place, SPAT)
        fetch.wait()
        rows = buf_ref[place]
        if t < 2:
            gain = (q_gain_ref, k_gain_ref)[t][pl.ds(spat[r], 1)]
            rows = (rows.astype(F32) * factors[t] * gain).astype(BF16)
        if t == 0:
            qs_ref[r] = rows
        else:
            kvs_ref[t - 1, r] = rows


def dot_t(a, b):
    return lax.dot_general(a, b, (((1,), (1,)), ((), ())), preferred_element_type=F32)


def attend(q, blocks, scores_ref, bias_of):
    top = None
    for w, (k, _) in enumerate(blocks):
        scores = bias_of(w, dot_t(q, k()) * SCALE)
        scores_ref[w] = scores
        block_top = jnp.maximum(scores[:, :SIZE], scores[:, SIZE:])
        top = block_top if top is None else jnp.maximum(top, block_top)
    top = jnp.max(top, axis=1, keepdims=True)
    total = jnp.zeros((POS, SIZE), F32)
    out = jnp.zeros((POS, SIZE), F32)
    for w, (_, v) in enumerate(blocks):
        expo = jnp.exp2(scores_ref[w] - top)
        total = total + expo[:, :SIZE] + expo[:, SIZE:]
        out = out + jnp.dot(expo.astype(BF16), v(), preferred_element_type=F32)
    return (out / jnp.sum(total, axis=1, keepdims=True)).astype(BF16)


def temporal_kernel(x_ref, out_ref, y_ref, sems):
    sends = []
    query_row = lax.broadcasted_iota(jnp.int32, (POS, POS), 0) % SUB
    key_row = lax.broadcasted_iota(jnp.int32, (POS, POS), 1) % SUB
    bias = jnp.where(query_row == key_row, 0.0, UNSEEN)
    for head in range(TEMP):
        q, k, v = (x_ref[:, t * TEMP + head].reshape(POS, SIZE) for t in range(3))
        scores = dot_t(q, k) * SCALE + bias
        expo = jnp.exp2(scores - jnp.max(scores, axis=1, keepdims=True))
        total = jnp.sum(expo, axis=1, keepdims=True)
        out = jnp.dot(expo.astype(BF16), v, preferred_element_type=F32) / total
        y_ref[head, :, 0] = out.astype(BF16).reshape(FRAMES, SUB, SIZE)
        sends.append(pltpu.make_async_copy(y_ref.at[head], out_ref.at[:, pl.ds(head, 1)], sems.at[head]))
        sends[-1].start()
    for send in sends:
        send.wait()


def spatial_kernel(order_ref, bias_ref, q_ref, *refs):
    kv_refs, (out_ref, scores_ref, rows_ref, sems) = refs[:NB], refs[NB:]

    def bias_of(w, scores):
        tiles = [
            scores[a * TILE : (a + 1) * TILE] + bias_ref[a : a + 1, w * POS : (w + 1) * POS] for a in range(NT)
        ]
        return jnp.concatenate(tiles, axis=0)

    copies = []
    for head in range(SPAT):
        blocks = [(lambda ref=ref: ref[0, head], lambda ref=ref: ref[1, head]) for ref in kv_refs]
        rows_ref[head] = attend(q_ref[head], blocks, scores_ref, bias_of)
        copies.append(pltpu.make_async_copy(rows_ref.at[head], out_ref.at[order_ref[head]], sems.at[head]))
        copies[-1].start()
    for copy in copies:
        copy.wait()


def join_kernel(order_ref, moved_ref, spatial_ref, out_ref, rows_ref, sems):
    copies = []
    for head in range(TEMP):
        rows_ref[head] = moved_ref[:, head].reshape(POS, SIZE)
        place = order_ref[SPAT + head]
        copies.append(pltpu.make_async_copy(rows_ref.at[head], out_ref.at[place], sems.at[head]))
        copies[-1].start()
    for copy in copies:
        copy.wait()


def route(block, target):
    pairs = [(i, target(i)) for i in range(FRAMES) if 0 <= target(i) < FRAMES]
    return lax.ppermute(block, "ctx", pairs)


def first_window(own):
    below = route(own, lambda i: i + 2)
    above = route(own, lambda i: i - 2)
    twin = route(own, lambda i: i ^ 1)
    return below, above, twin


def rest_window(own, below, above, twin):
    passed = jnp.where(lax.axis_index("ctx") % 2 == 1, below, above)
    passed, below, above = lax.optimization_barrier((passed, below, above))
    far = route(passed, lambda i: i + 1 if i % 2 else i - 1)
    return [far, below, route(below, lambda i: i ^ 1), own, twin, above, route(above, lambda i: i ^ 1)]


EVEN = (-3, -2, -1, 0, 1, 2, 3)
ODD = (3, -2, -3, 0, -1, 2, 1)


def bias_rows(neighbours, tiles):
    frame = lax.axis_index("ctx")
    offsets = jnp.where(frame % 2 == 0, jnp.array(EVEN, jnp.int32), jnp.array(ODD, jnp.int32))
    listed = (neighbours[0][None, :] == (frame + offsets)[:, None]).astype(jnp.int32)
    times = jnp.sum(listed[:, :, None, None] * tiles[0][None], axis=1)
    bias = jnp.where(times > 0, jnp.log2(jnp.maximum(times, 1).astype(F32)), UNSEEN)
    bias = jnp.repeat(jnp.transpose(bias, (1, 0, 2)), TILE, axis=2)
    return bias.reshape(NT, NB * POS)


def head_order(head_class):
    heads = jnp.arange(GROUP, dtype=jnp.int32)
    rank_key = head_class * GROUP + heads
    rank = jnp.sum((rank_key[None, :] < rank_key[:, None]).astype(jnp.int32), axis=1)
    return jnp.sum(jnp.where(rank[:, None] == heads[None, :], heads[:, None], 0), axis=0)


def bf16(*dims):
    return jax.ShapeDtypeStruct(dims, BF16)


def params(mib=32):
    return pltpu.CompilerParams(vmem_limit_bytes=mib * 1024 * 1024)


def swap_all(block):
    return lax.all_to_all(block, "ctx", split_axis=0, concat_axis=0, tiled=True)


def shards(query, key, value, query_gain, key_gain, head_class, neighbours, tiles):
    q, k, v = (jnp.transpose(a, (1, 0, 2)) for a in (query, key, value))
    sums = pl.pallas_call(
        sums_kernel,
        out_shape=jax.ShapeDtypeStruct((2, POS), F32),
        in_specs=[whole(pl.ANY)] * 2,
        out_specs=whole(),
        scratch_shapes=[
            pltpu.VMEM((GROUP, POS, SIZE), BF16),
            pltpu.VMEM((GROUP, POS, SIZE), BF16),
            pltpu.SemaphoreType.DMA((4 * GROUP,)),
        ],
        compiler_params=params(60),
        name="sums",
    )(q, k)
    sums = lax.psum(sums, "head")
    norm_specs = [whole(pltpu.SMEM)] + [whole()] * 3 + [whole(pl.ANY)] * 3
    chunk = pl.pallas_call(
        norm_temporal_kernel,
        out_shape=bf16(FRAMES, 3 * TEMP, SUB, SIZE),
        in_specs=[whole(pltpu.SMEM)] + [whole(pl.ANY)] * 6,
        out_specs=whole(pl.ANY),
        scratch_shapes=[
            pltpu.VMEM((2, POS), F32),
            pltpu.VMEM((GROUP, SIZE), F32),
            pltpu.VMEM((GROUP, SIZE), F32),
            pltpu.VMEM((3 * TEMP, POS, SIZE), BF16),
            pltpu.VMEM((3, FRAMES, TEMP, SUB, SIZE), BF16),
            pltpu.SemaphoreType.DMA((3 * TEMP,)),
            pltpu.SemaphoreType.DMA((3,)),
            pltpu.SemaphoreType.DMA((3,)),
        ],
        compiler_params=params(60),
        name="norm_temporal",
    )(head_class, sums, query_gain, key_gain, q, k, v)
    chunk, sums = lax.optimization_barrier((chunk, sums))
    rows = swap_all(chunk)
    q_own, kv_own = pl.pallas_call(
        norm_spatial_kernel,
        out_shape=(bf16(SPAT, POS, SIZE), bf16(2, SPAT, POS, SIZE)),
        in_specs=norm_specs,
        out_specs=(whole(),) * 2,
        scratch_shapes=[pltpu.VMEM((3 * SPAT, POS, SIZE), BF16), pltpu.SemaphoreType.DMA((3 * SPAT,))],
        compiler_params=params(16),
        name="norm_spatial",
    )(head_class, sums, query_gain, key_gain, q, k, v)
    first = first_window(kv_own)
    outputs = pl.pallas_call(
        temporal_kernel,
        out_shape=bf16(FRAMES, TEMP, SUB, SIZE),
        in_specs=[whole()],
        out_specs=whole(pl.ANY),
        scratch_shapes=[
            pltpu.VMEM((TEMP, FRAMES, 1, SUB, SIZE), BF16),
            pltpu.SemaphoreType.DMA((TEMP,)),
        ],
        compiler_params=params(16),
        name="temporal",
    )(rows)
    outputs, first = lax.optimization_barrier((outputs, first))
    temporal_out = swap_all(outputs)
    window = rest_window(kv_own, *first)

    order = head_order(head_class)
    bias = bias_rows(neighbours, tiles)
    smem = whole(pltpu.SMEM)
    spatial = pl.pallas_call(
        spatial_kernel,
        out_shape=bf16(GROUP, POS, SIZE),
        in_specs=[smem] + [whole()] * (2 + NB),
        out_specs=whole(pl.ANY),
        scratch_shapes=[
            pltpu.VMEM((NB, POS, POS), F32),
            pltpu.VMEM((SPAT, POS, SIZE), BF16),
            pltpu.SemaphoreType.DMA((SPAT,)),
        ],
        compiler_params=params(16),
        name="spatial",
    )(order, bias, q_own, *window)
    out = pl.pallas_call(
        join_kernel,
        out_shape=bf16(GROUP, POS, SIZE),
        in_specs=[smem, whole(), whole(pl.ANY)],
        out_specs=whole(pl.ANY),
        scratch_shapes=[pltpu.VMEM((TEMP, POS, SIZE), BF16), pltpu.SemaphoreType.DMA((TEMP,))],
        input_output_aliases={2: 0},
        compiler_params=params(16),
        name="join",
    )(order, temporal_out, spatial)
    return jnp.transpose(out, (1, 0, 2))


def solution(mesh):
    in_specs = (
        P("ctx", "head", None),
        P("ctx", "head", None),
        P("ctx", "head", None),
        P("head", None),
        P("head", None),
        P("head"),
        P("ctx", None),
        P("ctx", None, None, None),
    )
    out_specs = P("ctx", "head", None)
    return jax.shard_map(shards, mesh=mesh, in_specs=in_specs, out_specs=out_specs, check_vma=False)
```

```python
import jax
import jax.numpy as jnp
from jax import lax
from jax.experimental import pallas as pl
from jax.experimental.pallas import tpu as pltpu
from jax.sharding import PartitionSpec as P

SIZE = 128
GROUP = 5
TEMP = 2
SPAT = GROUP - TEMP
POS = 256
NB = 7
TILE = 64
NT = 4
FRAMES = 128
HEADS = 20
N_HEAD = HEADS // GROUP
LOG2E = 1.4426950408889634
SCALE = SIZE ** (-0.5) * LOG2E
UNSEEN = -1e30
BF16 = jnp.bfloat16
F32 = jnp.float32

SUB = POS // FRAMES


def whole(memory_space=pltpu.VMEM):
    return pl.BlockSpec(memory_space=memory_space)


def sorted_heads(class_ref):
    spat, temp = [0] * SPAT, [0] * TEMP
    n_spat, n_temp = 0, 0
    for head in range(GROUP):
        kind = class_ref[head]
        for r in range(SPAT):
            spat[r] = jnp.where((kind == 0) & (n_spat == r), head, spat[r])
        for r in range(TEMP):
            temp[r] = jnp.where((kind != 0) & (n_temp == r), head, temp[r])
        n_spat = n_spat + jnp.where(kind == 0, 1, 0)
        n_temp = n_temp + jnp.where(kind == 0, 0, 1)
    return spat, temp


def sums_kernel(q_ref, k_ref, sums_ref, q_buf, k_buf, sems):
    half = POS // 2
    fetches = []
    for row, (x_ref, x_buf) in enumerate(((q_ref, q_buf), (k_ref, k_buf))):
        for head in range(GROUP):
            for part in range(2):
                rows = pl.ds(part * half, half)
                sem = sems.at[(row * GROUP + head) * 2 + part]
                fetches.append(pltpu.make_async_copy(x_ref.at[head, rows], x_buf.at[head, rows], sem))
                fetches[-1].start()
    for row, x_buf in enumerate((q_buf, k_buf)):
        total = jnp.zeros((POS, SIZE), F32)
        for head in range(GROUP):
            for part in range(2):
                fetches[(row * GROUP + head) * 2 + part].wait()
            part = x_buf[head].astype(F32)
            total = total + part * part
        sums = jnp.sum(total.T, axis=0, keepdims=True)
        for member in range(N_HEAD):
            sums_ref[member, row : row + 1] = sums


def fetched(refs, heads, buf_ref, sems):
    fetches = []
    for t, x_ref in enumerate(refs):
        for r, head in enumerate(heads):
            place = t * len(heads) + r
            fetches.append(pltpu.make_async_copy(x_ref.at[head], buf_ref.at[place], sems.at[place]))
            fetches[-1].start()
    return fetches


def factors_of(sums_ref):
    factors = lax.rsqrt(jnp.sum(sums_ref[...], axis=0) / (HEADS * SIZE) + 1e-06)
    return [jnp.broadcast_to(factors[row : row + 1], (SIZE, POS)).T for row in range(2)]


def norm_temporal_kernel(class_ref, sums_ref, q_gain_ref, k_gain_ref, q_ref, k_ref, v_ref, chunk_ref, buf_ref, sems):
    _, temp = sorted_heads(class_ref)
    fetches = fetched((q_ref, k_ref, v_ref), temp, buf_ref, sems)
    factors = factors_of(sums_ref)
    for place, fetch in enumerate(fetches):
        t, r = divmod(place, TEMP)
        fetch.wait()
        rows = buf_ref[place]
        if t < 2:
            gain = (q_gain_ref, k_gain_ref)[t][pl.ds(temp[r], 1)]
            rows = (rows.astype(F32) * factors[t] * gain).astype(BF16)
        chunk_ref[:, place] = rows.reshape(FRAMES, SUB, SIZE)


def norm_spatial_kernel(
    class_ref, sums_ref, q_gain_ref, k_gain_ref, q_ref, k_ref, v_ref, qs_ref, kvs_ref, buf_ref, sems
):
    spat, _ = sorted_heads(class_ref)
    fetches = fetched((q_ref, k_ref, v_ref), spat, buf_ref, sems)
    factors = factors_of(sums_ref)
    for place, fetch in enumerate(fetches):
        t, r = divmod(place, SPAT)
        fetch.wait()
        rows = buf_ref[place]
        if t < 2:
            gain = (q_gain_ref, k_gain_ref)[t][pl.ds(spat[r], 1)]
            rows = (rows.astype(F32) * factors[t] * gain).astype(BF16)
        if t == 0:
            qs_ref[r] = rows
        else:
            kvs_ref[t - 1, r] = rows


def dot_t(a, b):
    return lax.dot_general(a, b, (((1,), (1,)), ((), ())), preferred_element_type=F32)


def attend(q, blocks, scores_ref, bias_of):
    top = None
    for w, (k, _) in enumerate(blocks):
        scores = bias_of(w, dot_t(q, k()) * SCALE)
        scores_ref[w] = scores
        block_top = jnp.maximum(scores[:, :SIZE], scores[:, SIZE:])
        top = block_top if top is None else jnp.maximum(top, block_top)
    top = jnp.max(top, axis=1, keepdims=True)
    total = jnp.zeros((POS, SIZE), F32)
    out = jnp.zeros((POS, SIZE), F32)
    for w, (_, v) in enumerate(blocks):
        expo = jnp.exp2(scores_ref[w] - top)
        total = total + expo[:, :SIZE] + expo[:, SIZE:]
        out = out + jnp.dot(expo.astype(BF16), v(), preferred_element_type=F32)
    return (out / jnp.sum(total, axis=1, keepdims=True)).astype(BF16)


def temporal_kernel(x_ref, y_ref):
    query_row = lax.broadcasted_iota(jnp.int32, (POS, POS), 0) % SUB
    key_row = lax.broadcasted_iota(jnp.int32, (POS, POS), 1) % SUB
    bias = jnp.where(query_row == key_row, 0.0, UNSEEN)
    for head in range(TEMP):
        q, k, v = (x_ref[:, t * TEMP + head].reshape(POS, SIZE) for t in range(3))
        scores = dot_t(q, k) * SCALE + bias
        expo = jnp.exp2(scores - jnp.max(scores, axis=1, keepdims=True))
        total = jnp.sum(expo, axis=1, keepdims=True)
        out = jnp.dot(expo.astype(BF16), v, preferred_element_type=F32) / total
        y_ref[:, head] = out.astype(BF16).reshape(FRAMES, SUB, SIZE)


def spatial_kernel(order_ref, bias_ref, q_ref, *refs):
    kv_refs, (out_ref, scores_ref, rows_ref, sems) = refs[:NB], refs[NB:]

    def bias_of(w, scores):
        tiles = [
            scores[a * TILE : (a + 1) * TILE] + bias_ref[a : a + 1, w * POS : (w + 1) * POS] for a in range(NT)
        ]
        return jnp.concatenate(tiles, axis=0)

    copies = []
    for head in range(SPAT):
        blocks = [(lambda ref=ref: ref[0, head], lambda ref=ref: ref[1, head]) for ref in kv_refs]
        rows_ref[head] = attend(q_ref[head], blocks, scores_ref, bias_of)
        copies.append(pltpu.make_async_copy(rows_ref.at[head], out_ref.at[order_ref[head]], sems.at[head]))
        copies[-1].start()
    for copy in copies:
        copy.wait()


def join_kernel(order_ref, moved_ref, spatial_ref, out_ref, rows_ref, sems):
    copies = []
    for head in range(TEMP):
        rows_ref[head] = moved_ref[:, head].reshape(POS, SIZE)
        place = order_ref[SPAT + head]
        copies.append(pltpu.make_async_copy(rows_ref.at[head], out_ref.at[place], sems.at[head]))
        copies[-1].start()
    for copy in copies:
        copy.wait()


def route(block, target):
    pairs = [(i, target(i)) for i in range(FRAMES) if 0 <= target(i) < FRAMES]
    return lax.ppermute(block, "ctx", pairs)


def first_window(own):
    below = route(own, lambda i: i + 2)
    above = route(own, lambda i: i - 2)
    twin = route(own, lambda i: i ^ 1)
    return below, above, twin


def rest_window(own, below, above, twin):
    passed = jnp.where(lax.axis_index("ctx") % 2 == 1, below, above)
    passed, below, above = lax.optimization_barrier((passed, below, above))
    far = route(passed, lambda i: i + 1 if i % 2 else i - 1)
    return [far, below, route(below, lambda i: i ^ 1), own, twin, above, route(above, lambda i: i ^ 1)]


EVEN = (-3, -2, -1, 0, 1, 2, 3)
ODD = (3, -2, -3, 0, -1, 2, 1)


def bias_rows(neighbours, tiles):
    frame = lax.axis_index("ctx")
    offsets = jnp.where(frame % 2 == 0, jnp.array(EVEN, jnp.int32), jnp.array(ODD, jnp.int32))
    listed = (neighbours[0][None, :] == (frame + offsets)[:, None]).astype(jnp.int32)
    times = jnp.sum(listed[:, :, None, None] * tiles[0][None], axis=1)
    bias = jnp.where(times > 0, jnp.log2(jnp.maximum(times, 1).astype(F32)), UNSEEN)
    bias = jnp.repeat(jnp.transpose(bias, (1, 0, 2)), TILE, axis=2)
    return bias.reshape(NT, NB * POS)


def head_order(head_class):
    heads = jnp.arange(GROUP, dtype=jnp.int32)
    rank_key = head_class * GROUP + heads
    rank = jnp.sum((rank_key[None, :] < rank_key[:, None]).astype(jnp.int32), axis=1)
    return jnp.sum(jnp.where(rank[:, None] == heads[None, :], heads[:, None], 0), axis=0)


def bf16(*dims):
    return jax.ShapeDtypeStruct(dims, BF16)


def params(mib=32):
    return pltpu.CompilerParams(vmem_limit_bytes=mib * 1024 * 1024)


def swap_all(block):
    return lax.all_to_all(block, "ctx", split_axis=0, concat_axis=0, tiled=True)


def shards(query, key, value, query_gain, key_gain, head_class, neighbours, tiles):
    q, k, v = (jnp.transpose(a, (1, 0, 2)) for a in (query, key, value))
    sums = pl.pallas_call(
        sums_kernel,
        out_shape=jax.ShapeDtypeStruct((N_HEAD, 2, POS), F32),
        in_specs=[whole(pl.ANY)] * 2,
        out_specs=whole(),
        scratch_shapes=[
            pltpu.VMEM((GROUP, POS, SIZE), BF16),
            pltpu.VMEM((GROUP, POS, SIZE), BF16),
            pltpu.SemaphoreType.DMA((4 * GROUP,)),
        ],
        compiler_params=params(60),
        name="sums",
    )(q, k)
    sums = lax.all_to_all(sums, "head", split_axis=0, concat_axis=0, tiled=True)
    norm_specs = [whole(pltpu.SMEM)] + [whole()] * 3 + [whole(pl.ANY)] * 3
    chunk = pl.pallas_call(
        norm_temporal_kernel,
        out_shape=bf16(FRAMES, 3 * TEMP, SUB, SIZE),
        in_specs=norm_specs,
        out_specs=whole(),
        scratch_shapes=[pltpu.VMEM((3 * TEMP, POS, SIZE), BF16), pltpu.SemaphoreType.DMA((3 * TEMP,))],
        compiler_params=params(60),
        name="norm_temporal",
    )(head_class, sums, query_gain, key_gain, q, k, v)
    chunk, sums = lax.optimization_barrier((chunk, sums))
    rows = swap_all(chunk)
    q_own, kv_own = pl.pallas_call(
        norm_spatial_kernel,
        out_shape=(bf16(SPAT, POS, SIZE), bf16(2, SPAT, POS, SIZE)),
        in_specs=norm_specs,
        out_specs=(whole(),) * 2,
        scratch_shapes=[pltpu.VMEM((3 * SPAT, POS, SIZE), BF16), pltpu.SemaphoreType.DMA((3 * SPAT,))],
        compiler_params=params(16),
        name="norm_spatial",
    )(head_class, sums, query_gain, key_gain, q, k, v)
    first = first_window(kv_own)
    outputs = pl.pallas_call(
        temporal_kernel,
        out_shape=bf16(FRAMES, TEMP, SUB, SIZE),
        in_specs=[whole()],
        out_specs=whole(),
        compiler_params=params(16),
        name="temporal",
    )(rows)
    outputs, first = lax.optimization_barrier((outputs, first))
    temporal_out = swap_all(outputs)
    window = rest_window(kv_own, *first)

    order = head_order(head_class)
    bias = bias_rows(neighbours, tiles)
    smem = whole(pltpu.SMEM)
    spatial = pl.pallas_call(
        spatial_kernel,
        out_shape=bf16(GROUP, POS, SIZE),
        in_specs=[smem] + [whole()] * (2 + NB),
        out_specs=whole(pl.ANY),
        scratch_shapes=[
            pltpu.VMEM((NB, POS, POS), F32),
            pltpu.VMEM((SPAT, POS, SIZE), BF16),
            pltpu.SemaphoreType.DMA((SPAT,)),
        ],
        compiler_params=params(16),
        name="spatial",
    )(order, bias, q_own, *window)
    out = pl.pallas_call(
        join_kernel,
        out_shape=bf16(GROUP, POS, SIZE),
        in_specs=[smem, whole(), whole(pl.ANY)],
        out_specs=whole(pl.ANY),
        scratch_shapes=[pltpu.VMEM((TEMP, POS, SIZE), BF16), pltpu.SemaphoreType.DMA((TEMP,))],
        input_output_aliases={2: 0},
        compiler_params=params(16),
        name="join",
    )(order, temporal_out, spatial)
    return jnp.transpose(out, (1, 0, 2))


def solution(mesh):
    in_specs = (
        P("ctx", "head", None),
        P("ctx", "head", None),
        P("ctx", "head", None),
        P("head", None),
        P("head", None),
        P("head"),
        P("ctx", None),
        P("ctx", None, None, None),
    )
    out_specs = P("ctx", "head", None)
    return jax.shard_map(shards, mesh=mesh, in_specs=in_specs, out_specs=out_specs, check_vma=False)
```
